32 devices in a mesh: groups: 2 (over y), dp: 4 (over x, core), tensor: 4 (over z).
Axes of the slice: x: 2, y: 2, z: 4, core: 2. Of those that a mesh axis runs over, the one named last changes fastest.
Arguments:
- residual_in: bfloat16 [48, 12288], P(('groups', 'tensor'), 'dp'), parts along dimension 0, may hold values from -6 to 6
- norm_gain: float32 [12288], P('dp'), may hold values from 0.1 to 1.9
- query: bfloat16 [48, 6144], P(('groups', 'dp'), 'tensor'), parts along dimension 0, may hold values from -6 to 6
- new_key: bfloat16 [48, 6144], P(('groups', 'dp'), 'tensor'), parts along dimension 0, may hold values from -6 to 6
- new_value: bfloat16 [48, 6144], P(('groups', 'dp'), 'tensor'), parts along dimension 0, may hold values from -6 to 6
- key_cache: bfloat16 [48, 256, 6144], P(('groups', 'dp'), None, 'tensor'), parts along dimension 0, may hold values from -6 to 6
- value_cache: bfloat16 [48, 256, 6144], P(('groups', 'dp'), None, 'tensor'), parts along dimension 0, may hold values from -6 to 6
- cache_length: int32 [48], P(('groups', 'dp')), parts along dimension 0, may hold values from 1 to 256, as said below
- out_weight: bfloat16 [6144, 12288], P('tensor', 'dp'), may hold values from -0.75 to 0.75
- up_weight: bfloat16 [12288, 24576], P('dp', 'tensor'), may hold values from -0.0546875 to 0.0546875
- down_weight: bfloat16 [24576, 12288], P('tensor', 'dp'), may hold values from -0.09375 to 0.09375
- block_list: int32 [8, 24], P(('groups', 'tensor')), parts along dimension 0, may hold values from 0 to 47, as said below
- block_count: int32 [8], P(('groups', 'tensor')), parts along dimension 0, may hold values from 1 to 24, as said below
Outputs:
- mixed_out: bfloat16 [48, 12288], P(('groups', 'tensor'), 'dp'), parts along dimension 0
The draws below stay inside these ranges and needn't reach their ends.
There are 2 independent parts, one for each index of `groups`. The reference program is written for one: setup_inputs(seed, part) draws one part's arguments, and reference() takes and returns one part's arrays. A program takes and returns all parts, laid end to end along the dimension named above; an argument that names none is the same for every part. Nothing has to cross between parts.
Inputs may be any that keep to these rules, and one draw needn't show every extreme that they name: `cache_length`: some conversation in every draw has exactly 256 valid positions. `block_list`: the 24 entries of a shard's list are distinct blocks of that shard; entries past the count are padding. `block_count`: some shard in every draw lists exactly 24 active blocks.
All inputs are finite; a program needn't handle non-finite values.
Results may differ from the reference program's by a relative error of at most 0.0075.
Values may be sent and summed in bfloat16 or wider, within the bound.
No kernel may reach another device: no remote copies, remote signals or barrier semaphores. Data moves between devices by JAX's collectives and lax.ppermute only.
A program may use at most 192 MiB of HBM per device.

```python
import jax
import jax.numpy as jnp
from jax import lax

D = 12288
HEADS = 48
HDIM = 128
FF = 24576
BLOCK = 128
CACHE = 256
BATCH = 24
SHB = 48
MAXB = 24
N_TENSOR = 4


def draw_query(key, part):
    key = jax.random.fold_in(key, 21)
    base = jnp.clip(jax.random.normal(key, (BATCH, HEADS, HDIM)), -6.0, 6.0)
    return base.reshape(BATCH, HEADS * HDIM).astype(jnp.bfloat16)


def draw_new_key(key, part):
    key = jax.random.fold_in(key, 22)
    base = jnp.clip(jax.random.normal(key, (BATCH, HEADS, HDIM)), -6.0, 6.0)
    return base.reshape(BATCH, HEADS * HDIM).astype(jnp.bfloat16)


def draw_key_cache(key, part):
    key = jax.random.fold_in(key, 23)
    base = jnp.clip(jax.random.normal(key, (BATCH, CACHE, HEADS, HDIM)), -6.0, 6.0)
    return base.reshape(BATCH, CACHE, HEADS * HDIM).astype(jnp.bfloat16)


def draw_residual_in(key, part):
    key = jax.random.fold_in(key, 31)
    column = jnp.arange(D).astype(jnp.float32) / D
    base = jnp.clip(jax.random.normal(key, (BATCH, D)), -4.0, 4.0)
    values = base * 0.5 * (3.0 ** column)[None, :]
    return values.astype(jnp.bfloat16)


def draw_cache_length(key, part):
    key = jax.random.fold_in(key, 41)
    lengths = jax.random.randint(key, (BATCH,), 1, CACHE + 1)
    longest = jax.random.randint(jax.random.fold_in(key, 1), (), 0, BATCH)
    return lengths.at[longest].set(CACHE).astype(jnp.int32)


def draw_block_count(key, part):
    key = jax.random.fold_in(key, 51)
    counts = jax.random.randint(key, (N_TENSOR,), 1, SHB // 4 + 1)
    busiest = jax.random.randint(jax.random.fold_in(key, 1), (), 0, N_TENSOR)
    return counts.at[busiest].set(MAXB).astype(jnp.int32)


def draw_block_list(key, part):
    key = jax.random.fold_in(key, 61)
    shard_keys = jax.random.split(key, N_TENSOR)
    orders = jax.vmap(lambda single: jax.random.permutation(single, SHB))(shard_keys)
    return orders[:, :MAXB].astype(jnp.int32)


def block_scale(rng, dims, pieces, smallest, largest):
    def one(axis_at, blocks):
        heights = jax.random.uniform(jax.random.fold_in(jax.random.fold_in(rng, 6), axis_at), (blocks,), jnp.float32, smallest / len(pieces), largest / len(pieces))
        return jnp.repeat(jnp.exp(heights), dims[axis_at] // blocks).reshape((-1,) + (1,) * (len(dims) - axis_at - 1))

    loudness = one(*pieces[0])
    for cut in pieces[1:]:
        loudness = loudness * one(*cut)
    return loudness


def noise(own_key, dims, width, bound, pieces=(), kind=jnp.bfloat16):
    values = jax.random.normal(own_key, dims, jnp.float32) * width
    if len(pieces) > 0:
        values = block_scale(own_key, dims, pieces, -0.22, 0.18) * values
    return jnp.clip(values, min=-bound, max=bound).astype(kind)


def setup_inputs(seed: int = 0, part: int = 0) -> dict:
    splits = jax.random.split(jax.random.key(seed), 14)
    own_keys = jax.random.split(jax.random.fold_in(splits[13], part), 14)
    return {
        "residual_in": draw_residual_in(jax.random.fold_in(jax.random.fold_in(splits[13], part), 71), part),
        "norm_gain": jnp.clip(1.0 + 0.18 * jax.random.normal(splits[1], (D,), jnp.float32), 0.1, 1.9),
        "query": draw_query(jax.random.fold_in(jax.random.fold_in(splits[13], part), 71), part),
        "new_key": draw_new_key(jax.random.fold_in(jax.random.fold_in(splits[13], part), 71), part),
        "new_value": noise(own_keys[4], (BATCH, HEADS * HDIM), 1.0, 6.0, ((0, 4), (1, 4))),
        "key_cache": draw_key_cache(jax.random.fold_in(jax.random.fold_in(splits[13], part), 71), part),
        "value_cache": noise(own_keys[6], (BATCH, CACHE, HEADS * HDIM), 1.0, 6.0, ((0, 4), (2, 4))),
        "cache_length": draw_cache_length(jax.random.fold_in(jax.random.fold_in(splits[13], part), 71), part),
        "out_weight": noise(splits[8], (HEADS * HDIM, D), (4 * (HEADS * HDIM) ** -0.5), 0.75, ((0, 4), (1, 4))),
        "up_weight": noise(splits[9], (D, FF), D ** -0.5, 0.0546875, ((0, 4), (1, 4))),
        "down_weight": noise(splits[10], (FF, D), (FF // 6) ** -0.5, 0.09375, ((0, 4), (1, 4))),
        "block_list": draw_block_list(jax.random.fold_in(jax.random.fold_in(splits[13], part), 71), part),
        "block_count": draw_block_count(jax.random.fold_in(jax.random.fold_in(splits[13], part), 71), part),
    }


def attend(query, new_key, new_value, key_cache, value_cache, cache_length):
    batch = query.shape[0]
    heads = query.shape[1] // HDIM
    span = key_cache.shape[1]
    queries = query.astype(jnp.float32).reshape(batch, heads, HDIM)
    keys_old = key_cache.astype(jnp.float32).reshape(batch, span, heads, HDIM)
    values_old = value_cache.astype(jnp.float32).reshape(batch, span, heads, HDIM)
    keys_new = new_key.astype(jnp.float32).reshape(batch, heads, HDIM)
    values_new = new_value.astype(jnp.float32).reshape(batch, heads, HDIM)
    factor = HDIM ** (-0.5)
    scores = jnp.einsum('bhd,bphd->bhp', queries, keys_old) * factor
    self_score = lax.optimization_barrier(jnp.sum(queries * keys_new, axis=-1)) * factor
    position = jnp.arange(span, dtype=jnp.int32)
    visible = position[None, :] < cache_length.astype(jnp.int32)[:, None]
    scores = jnp.where(visible[:, None, :], scores, -1e+30)
    highest = jnp.maximum(lax.optimization_barrier(jnp.max(scores, axis=-1)), self_score)
    weights_old = jnp.exp(scores - highest[..., None])
    weight_self = jnp.exp(self_score - highest)
    denominator = lax.optimization_barrier(jnp.sum(weights_old, axis=-1)) + weight_self
    rounded_old = lax.optimization_barrier(weights_old.astype(jnp.bfloat16)).astype(jnp.float32)
    rounded_self = lax.optimization_barrier(weight_self.astype(jnp.bfloat16)).astype(jnp.float32)
    combined = jnp.einsum('bhp,bphd->bhd', rounded_old, values_old) + rounded_self[..., None] * values_new
    return (combined / denominator[..., None]).astype(jnp.bfloat16).reshape(batch, heads * HDIM)

def normalize(widened, total, squares, norm_gain):
    center = total / D
    spread = squares / D - center * center
    scaled = (widened - center[:, None]) * lax.rsqrt(spread + 1e-05)[:, None]
    return (scaled * norm_gain[None, :]).astype(jnp.bfloat16)

def reference(residual_in, norm_gain, query, new_key, new_value, key_cache, value_cache, cache_length, out_weight, up_weight, down_weight, block_list, block_count):
    heads_out = attend(query, new_key, new_value, key_cache, value_cache, cache_length)
    hidden = (residual_in.astype(jnp.float32) + jnp.dot(heads_out, out_weight, preferred_element_type=jnp.float32)).astype(jnp.bfloat16)
    widened = hidden.astype(jnp.float32)
    normed = normalize(widened, lax.optimization_barrier(jnp.sum(widened, axis=1)), lax.optimization_barrier(jnp.sum(widened * widened, axis=1)), norm_gain)
    pre = jnp.dot(normed, up_weight, preferred_element_type=jnp.float32)
    slot_mask = jnp.arange(MAXB, dtype=jnp.int32)[None, :] < block_count.astype(jnp.int32)[:, None]
    matches = (block_list.astype(jnp.int32)[:, :, None] == jnp.arange(SHB, dtype=jnp.int32)[None, None, :]) & slot_mask[:, :, None]
    active = jnp.any(matches, axis=1).astype(jnp.float32).reshape(N_TENSOR * SHB)
    column_mask = jnp.repeat(active, BLOCK)
    act = (jnp.maximum(pre, 0.0) * column_mask[None, :]).astype(jnp.bfloat16)
    return (widened + jnp.dot(act, down_weight, preferred_element_type=jnp.float32)).astype(jnp.bfloat16)
```

```python
import functools

import jax
import jax.numpy as jnp
from jax import lax
from jax.experimental import pallas as pl
from jax.experimental.pallas import tpu as pltpu
from jax.sharding import PartitionSpec as P

D = 12288
HDIM = 128
BLOCK = 128
ROWS = 8
TILE = 256
MIB = 1 << 20

F32 = jnp.float32
BF16 = jnp.bfloat16

IN_VMEM = pl.BlockSpec(memory_space=pltpu.VMEM)
IN_SMEM = pl.BlockSpec(memory_space=pltpu.SMEM)
ANYWHERE = pl.BlockSpec(memory_space=pl.ANY)


def dot(left, right):
    return jnp.dot(left, right, preferred_element_type=F32)


def pad_rows(value, rows):
    missing = rows - value.shape[0]
    if missing == 0:
        return value
    return jnp.concatenate([value, jnp.zeros((missing, value.shape[1]), value.dtype)], axis=0)


def spread_rows(value, count):
    each = value.shape[0] // count
    groups = [pad_rows(value[i * each : (i + 1) * each], ROWS) for i in range(count)]
    return jnp.concatenate(groups, axis=0)


def compact_rows(value, count, each):
    return jnp.concatenate([value[i * ROWS : i * ROWS + each] for i in range(count)], axis=0)


def column_tiles(width):
    return [(low, min(TILE, width - low)) for low in range(0, width, TILE)]


def attend_kernel(
    length, query, new_key, new_value, keys, values, weight, out, weight_out,
    key_buf, value_buf, weights_buf, own_buf, total_buf, sems,
):
    batch, span, width = key_buf.shape
    heads = width // HDIM
    lines = weights_buf.shape[0] // batch
    factor = HDIM ** (-0.5)
    key_copies = [
        pltpu.make_async_copy(keys.at[b], key_buf.at[b], sems.at[0, b]) for b in range(batch)
    ]
    value_copies = [
        pltpu.make_async_copy(values.at[b], value_buf.at[b], sems.at[1, b]) for b in range(batch)
    ]
    weight_copy = pltpu.make_async_copy(weight, weight_out, sems.at[2, 0])
    for copy in key_copies + value_copies + [weight_copy]:
        copy.start()
    row = lax.broadcasted_iota(jnp.int32, (lines, width), 0)
    column = lax.broadcasted_iota(jnp.int32, (lines, width), 1)
    mine = (column // HDIM) == row
    position = lax.broadcasted_iota(jnp.int32, (lines, span), 1)
    for b in range(batch):
        one = query[b : b + 1, :].astype(F32)
        picked = jnp.where(mine, one, 0.0)
        own = jnp.sum(picked * new_key[b : b + 1, :].astype(F32), axis=1, keepdims=True) * factor
        own_buf[b * lines : (b + 1) * lines, :] = jnp.broadcast_to(own, (lines, HDIM))
        key_copies[b].wait()
        scores = lax.dot_general(
            picked.astype(BF16), key_buf[b], (((1,), (1,)), ((), ())), preferred_element_type=F32
        )
        scores = jnp.where(position < length[b], scores * factor, -1e30)
        weights_buf[b * lines : (b + 1) * lines, :] = scores
    scores = weights_buf[...]
    own = own_buf[:, 0:1]
    highest = jnp.maximum(jnp.max(scores, axis=1, keepdims=True), own)
    weights = jnp.exp(scores - highest)
    own_weight = jnp.exp(own - highest)
    total = jnp.sum(weights, axis=1, keepdims=True) + own_weight
    weights_buf[...] = weights
    own_buf[...] = jnp.broadcast_to(own_weight.astype(BF16).astype(F32), own_buf.shape)
    total_buf[...] = jnp.broadcast_to(total, total_buf.shape)
    rows = []
    for b in range(batch):
        at = slice(b * lines, (b + 1) * lines)
        value_copies[b].wait()
        combined = dot(weights_buf[at, :].astype(BF16), value_buf[b])
        combined = combined + own_buf[at, 0:1] * new_value[b : b + 1, :].astype(F32)
        combined = jnp.where(mine, combined / total_buf[at, 0:1], 0.0)
        rows.append(jnp.sum(combined, axis=0, keepdims=True))
    out[...] = pad_rows(jnp.concatenate(rows, axis=0), ROWS).astype(BF16)
    weight_copy.wait()


def attend(query, new_key, new_value, key_cache, value_cache, cache_length, out_weight):
    batch, span, width = key_cache.shape
    lines = -(-(width // HDIM) // 16) * 16
    read = 2 * (key_cache.size + value_cache.size + out_weight.size)
    return pl.pallas_call(
        attend_kernel,
        out_shape=(
            jax.ShapeDtypeStruct((ROWS, width), BF16),
            pltpu.VMEM(out_weight.shape, BF16),
        ),
        in_specs=[IN_SMEM, IN_VMEM, IN_VMEM, IN_VMEM, ANYWHERE, ANYWHERE, ANYWHERE],
        out_specs=(IN_VMEM, IN_VMEM),
        scratch_shapes=[
            pltpu.VMEM(key_cache.shape, BF16),
            pltpu.VMEM(value_cache.shape, BF16),
            pltpu.VMEM((batch * lines, span), F32),
            pltpu.VMEM((batch * lines, HDIM), F32),
            pltpu.VMEM((batch * lines, HDIM), F32),
            pltpu.SemaphoreType.DMA((3, batch)),
        ],
        compiler_params=pltpu.CompilerParams(vmem_limit_bytes=36 * MIB),
        cost_estimate=pl.CostEstimate(
            flops=4 * batch * lines * span * width, bytes_accessed=read, transcendentals=0
        ),
        name="attend",
    )(cache_length, query, new_key, new_value, key_cache, value_cache, out_weight)


def fetch_kernel(jobs, picks, after, up, down, *rest):
    outs, sem = rest[:-1], rest[-1]
    copies = []
    for out, (which, first, count) in zip(outs, jobs):
        for j in range(count):
            start = pl.multiple_of(picks[first + j] * BLOCK, BLOCK)
            place = pl.ds(j * BLOCK, BLOCK)
            if which == "up":
                copy = pltpu.make_async_copy(up.at[:, pl.ds(start, BLOCK)], out.at[:, place], sem)
            else:
                copy = pltpu.make_async_copy(down.at[pl.ds(start, BLOCK), :], out.at[place, :], sem)
            copy.start()
            copies.append(copy)
    for copy in copies:
        copy.wait()


def fetch(jobs, picks, after, up_weight, down_weight, name):
    shapes = []
    for which, _, count in jobs:
        if which == "up":
            shapes.append((up_weight.shape[0], count * BLOCK))
        else:
            shapes.append((count * BLOCK, down_weight.shape[1]))
    size = sum(2 * a * b for a, b in shapes)
    return pl.pallas_call(
        functools.partial(fetch_kernel, jobs),
        out_shape=tuple(pltpu.VMEM(shape, BF16) for shape in shapes),
        in_specs=[IN_SMEM, ANYWHERE, ANYWHERE, ANYWHERE],
        out_specs=tuple(IN_VMEM for _ in shapes),
        scratch_shapes=[pltpu.SemaphoreType.DMA],
        compiler_params=pltpu.CompilerParams(vmem_limit_bytes=size + 4 * MIB),
        cost_estimate=pl.CostEstimate(flops=0, bytes_accessed=2 * size, transcendentals=0),
        name=name,
    )(picks, after, up_weight, down_weight)


def project_kernel(dp_count, batch, tensor_count, place, *refs):
    heads, weight = refs[:dp_count], refs[dp_count]
    outs = refs[dp_count + 1 : dp_count + 1 + tensor_count]
    gathered, result = refs[dp_count + 1 + tensor_count :]
    for k in range(dp_count):
        source = lax.rem(place[0] - k + dp_count, dp_count)
        gathered[pl.ds(pl.multiple_of(source * ROWS, ROWS), ROWS), :] = heads[k][...].astype(F32)
    each = batch // dp_count
    full = gathered[...]
    if dp_count != tensor_count:
        full = spread_rows(compact_rows(full, dp_count, each), tensor_count)
    full = full.astype(BF16)
    for low, size in column_tiles(weight.shape[1]):
        result[:, low : low + size] = dot(full, weight[:, low : low + size])
    for k in range(tensor_count):
        target = lax.rem(place[1] + k, tensor_count)
        part = result[pl.ds(pl.multiple_of(target * ROWS, ROWS), ROWS), :]
        outs[k][...] = part.astype(outs[k].dtype)


def group_shapes(count, width):
    return tuple(
        jax.ShapeDtypeStruct((ROWS, width), F32 if k == 0 else BF16) for k in range(count)
    )


def project(place, heads, weight, batch, tensor_count):
    dp_count = len(heads)
    depth, width = weight.shape
    return pl.pallas_call(
        functools.partial(project_kernel, dp_count, batch, tensor_count),
        out_shape=group_shapes(tensor_count, width),
        in_specs=[IN_SMEM] + [IN_VMEM] * (dp_count + 1),
        out_specs=(IN_VMEM,) * tensor_count,
        scratch_shapes=[
            pltpu.VMEM((dp_count * ROWS, depth), F32),
            pltpu.VMEM((tensor_count * ROWS, width), F32),
        ],
        compiler_params=pltpu.CompilerParams(vmem_limit_bytes=24 * MIB),
        cost_estimate=pl.CostEstimate(
            flops=2 * batch * depth * width, bytes_accessed=2 * depth * width, transcendentals=0
        ),
        name="project",
    )(place, *heads, weight)


def center_kernel(tensor_count, each, place, *refs):
    hidden, gain = refs[:tensor_count], refs[tensor_count]
    rows_out, sums_out, gathered = refs[tensor_count + 1 :]
    for k in range(tensor_count):
        source = lax.rem(place[1] - k + tensor_count, tensor_count)
        gathered[pl.ds(pl.multiple_of(source * ROWS, ROWS), ROWS), :] = hidden[k][...].astype(F32)
    rows = compact_rows(gathered[...], tensor_count, each)
    batch, width = rows.shape
    total = jnp.sum(rows, axis=1, keepdims=True)
    squares = jnp.sum(rows * rows, axis=1, keepdims=True)
    lane = lax.broadcasted_iota(jnp.int32, sums_out.shape, 1)
    sums_out[...] = jnp.where(lane == 0, total, squares)
    scale = gain[...]
    scaled = (rows - total * (1.0 / width)) * scale
    high = scale.astype(BF16).astype(F32)
    full = jnp.concatenate([scaled, high, scale - high], axis=0)
    rows_out[...] = pad_rows(full, rows_out.shape[0]).astype(BF16)


def center(place, hidden, gain, each):
    tensor_count = len(hidden)
    batch = each * tensor_count
    width = hidden[0].shape[1]
    lines = -(-(batch + 2) // 16) * 16
    return pl.pallas_call(
        functools.partial(center_kernel, tensor_count, each),
        out_shape=(
            jax.ShapeDtypeStruct((lines, width), BF16),
            jax.ShapeDtypeStruct((batch, 128), F32),
        ),
        in_specs=[IN_SMEM] + [IN_VMEM] * (tensor_count + 1),
        out_specs=(IN_VMEM, IN_VMEM),
        scratch_shapes=[pltpu.VMEM((tensor_count * ROWS, width), F32)],
        compiler_params=pltpu.CompilerParams(vmem_limit_bytes=16 * MIB),
        name="center",
    )(place, *hidden, gain.reshape(1, width))


def up_kernel(parts, rows, *refs):
    out = refs[parts]
    base = 0
    for weight in refs[:parts]:
        for low, size in column_tiles(weight.shape[1]):
            out[:, base + low : base + low + size] = dot(rows[...], weight[:, low : low + size])
        base += weight.shape[1]


def up_product(rows, weights):
    width = sum(weight.shape[1] for weight in weights)
    lines, depth = rows.shape
    return pl.pallas_call(
        functools.partial(up_kernel, len(weights)),
        out_shape=jax.ShapeDtypeStruct((lines, width), F32),
        in_specs=[IN_VMEM] * (1 + len(weights)),
        out_specs=IN_VMEM,
        compiler_params=pltpu.CompilerParams(vmem_limit_bytes=24 * MIB),
        cost_estimate=pl.CostEstimate(
            flops=2 * lines * depth * width, bytes_accessed=2 * depth * width, transcendentals=0
        ),
        name="up_product",
    )(rows, *weights)


def down_kernel(parts, others, tensor_count, place, near, *refs):
    far, weights = refs[:others], refs[others : others + parts]
    outs, result = refs[others + parts : -1], refs[-1]
    total = near[...]
    for other in far:
        total = total + other[...].astype(F32)
    lane = lax.broadcasted_iota(jnp.int32, total.shape, 1)
    act = jnp.where(lane < place[2] * BLOCK, jnp.maximum(total, 0.0), 0.0)
    act = spread_rows(act, tensor_count).astype(BF16)
    for low, size in column_tiles(weights[0].shape[1]):
        base = 0
        summed = None
        for weight in weights:
            depth = weight.shape[0]
            term = dot(act[:, base : base + depth], weight[:, low : low + size])
            summed = term if summed is None else summed + term
            base += depth
        result[:, low : low + size] = summed
    for k in range(tensor_count):
        target = lax.rem(place[1] + k, tensor_count)
        part = result[pl.ds(pl.multiple_of(target * ROWS, ROWS), ROWS), :]
        outs[k][...] = part.astype(outs[k].dtype)


def down_product(place, near, far, weights, tensor_count):
    width = weights[0].shape[1]
    depth = near.shape[1]
    return pl.pallas_call(
        functools.partial(down_kernel, len(weights), len(far), tensor_count),
        out_shape=group_shapes(tensor_count, width),
        in_specs=[IN_SMEM] + [IN_VMEM] * (1 + len(far) + len(weights)),
        out_specs=(IN_VMEM,) * tensor_count,
        scratch_shapes=[pltpu.VMEM((tensor_count * ROWS, width), F32)],
        compiler_params=pltpu.CompilerParams(vmem_limit_bytes=28 * MIB),
        cost_estimate=pl.CostEstimate(
            flops=2 * near.shape[0] * depth * width,
            bytes_accessed=2 * depth * width,
            transcendentals=0,
        ),
        name="down_product",
    )(place, near, *far, *weights)


def shift(value, axis, count, by):
    return lax.ppermute(value, axis, [(i, (i + by) % count) for i in range(count)])


def gather(value, axis, count):
    return [value] + [shift(value, axis, count, k) for k in range(1, count)]


def scatter(parts, axis, count):
    return [parts[0]] + [shift(parts[k], axis, count, k) for k in range(1, count)]


def shards(
    residual_in,
    norm_gain,
    query,
    new_key,
    new_value,
    key_cache,
    value_cache,
    cache_length,
    out_weight,
    up_weight,
    down_weight,
    block_list,
    block_count,
):
    dp_count = lax.axis_size("dp")
    tensor_count = lax.axis_size("tensor")
    each = residual_in.shape[0]
    batch = each * tensor_count
    width = residual_in.shape[1]
    picks = block_list[0]
    listed = picks.shape[0]
    place = jnp.stack(
        [lax.axis_index("dp"), lax.axis_index("tensor"), block_count[0]]
    ).astype(jnp.int32)

    heads, out_block = attend(
        query, new_key, new_value, key_cache, value_cache, cache_length, out_weight
    )
    first = listed // 2
    (up_a,) = fetch([("up", 0, first)], picks, heads, up_weight, down_weight, "fetch_a")
    gathered = gather(heads, "dp", dp_count)
    terms = project(place, gathered, out_block, batch, tensor_count)
    up_b, down_a = fetch(
        [("up", first, listed - first), ("down", 0, first)],
        picks, terms[1], up_weight, down_weight, "fetch_b",
    )
    arrived = scatter(terms, "tensor", tensor_count)
    padded = jnp.pad(residual_in, ((0, ROWS - each), (0, 0))).astype(F32)
    hidden = functools.reduce(lambda a, b: a + b.astype(F32), arrived, padded).astype(BF16)
    (down_b,) = fetch(
        [("down", first, listed - first)], picks, hidden, up_weight, down_weight, "fetch_c"
    )
    rows, sums = center(place, gather(hidden, "tensor", tensor_count), norm_gain, each)
    all_sums = functools.reduce(jnp.add, gather(sums, "dp", dp_count))
    product = up_product(rows, [up_a, up_b])
    middle = all_sums[:, 0:1] / D
    spread = all_sums[:, 1:2] / D - middle * middle
    offset = sums[:, 0:1] / width - middle
    pre = (product[:batch] + offset * (product[batch] + product[batch + 1])[None, :]) * lax.rsqrt(
        spread + 1e-05
    )
    near = pre + lax.ppermute(pre, "dp", [(i, i ^ 1) for i in range(dp_count)])
    sent = near.astype(BF16)
    far = [shift(sent, "dp", dp_count, 2 * k) for k in range(1, dp_count // 2)]
    parts = down_product(place, near, far, [down_a, down_b], tensor_count)
    feed = scatter(parts, "tensor", tensor_count)
    out = functools.reduce(lambda a, b: a + b.astype(F32), feed, hidden.astype(F32))
    return out[:each].astype(BF16)


def solution(mesh):
    return jax.shard_map(
        shards,
        mesh=mesh,
        in_specs=(
            P(("groups", "tensor"), "dp"),
            P("dp"),
            P(("groups", "dp"), "tensor"),
            P(("groups", "dp"), "tensor"),
            P(("groups", "dp"), "tensor"),
            P(("groups", "dp"), None, "tensor"),
            P(("groups", "dp"), None, "tensor"),
            P(("groups", "dp")),
            P("tensor", "dp"),
            P("dp", "tensor"),
            P("tensor", "dp"),
            P(("groups", "tensor"), None),
            P(("groups", "tensor")),
        ),
        out_specs=P(("groups", "tensor"), "dp"),
        check_vma=False,
    )
```
